256 devices in a mesh: dp: 8 (over z), tensor: 16 (over y, x), group: 2 (over core).
Axes of the slice: x: 4, y: 4, z: 8, core: 2. Of those that a mesh axis runs over, the one named last changes fastest.
Arguments:
- resid: bfloat16 [1024, 4096], P('dp'), may hold values from -6 to 6
- mixer_out: bfloat16 [1024, 8192], P('dp', ('tensor', 'group')), may hold values from -6 to 6
- out_proj: bfloat16 [8192, 4096], P(('tensor', 'group')), may hold values from -0.0625 to 0.0625
- norm_gain: float32 [4096], replicated, may hold values from 0.1 to 1.9
- router: float32 [4096, 8], replicated, may hold values from -0.09375 to 0.09375
- routes: int32 [1024, 2], P('dp'), may hold values from 0 to 7, all different within a row; in each aligned block of 128 rows (0 to 127, 128 to 255, ...) at most 48 rows name the same one
- w_gate: bfloat16 [16, 4096, 3584], P('tensor', None, ('dp', 'group')), may hold values from -0.09375 to 0.09375
- w_up: bfloat16 [16, 4096, 3584], P('tensor', None, ('dp', 'group')), may hold values from -0.09375 to 0.09375
- w_down: bfloat16 [16, 3584, 4096], P('tensor', ('dp', 'group')), may hold values from -0.0625 to 0.0625
- cotangent: bfloat16 [1024, 4096], P('dp'), may hold values from -6 to 6
Outputs:
- layer_out: bfloat16 [1024, 4096], P('dp')
- grad_mixer: bfloat16 [1024, 8192], P('dp', ('tensor', 'group'))
- grad_down: bfloat16 [16, 3584, 4096], P('tensor', ('dp', 'group'))
The draws below stay inside these ranges and needn't reach their ends.
Inputs may be any that keep to these rules, and one draw needn't show every extreme that they name: `routes`: in each aligned block of 128 rows (the tokens of one replica) no expert is named by more than 48 rows, and some expert reaches 48 in some block; the two experts of a row differ.
All inputs are finite; a program needn't handle non-finite values.
Results may differ from the reference program's by a relative error of at most 0.03.
Values may be sent and summed in bfloat16 or wider, within the bound.
No kernel may reach another device: no remote copies, remote signals or barrier semaphores. Data moves between devices by JAX's collectives and lax.ppermute only.
A program may use at most 128 MiB of HBM per device.

```python
import math
import jax
import jax.numpy as jnp
import numpy as np
from jax import lax

D = 4096
INNER = 8192
FF = 7168
TOK_DEV = 128
TOKENS = 1024
EXPERTS = 8
CH = 256
CAP = 48
N_DP = 8
N_TENSOR = 16
N_GROUP = 2


def level_of(rng, extent, shards, low, top_value):
    gain = 1.0
    for dim, blocks in shards:
        steps = jax.random.uniform(jax.random.fold_in(jax.random.fold_in(rng, 6), dim), (blocks,), jnp.float32, low / len(shards), top_value / len(shards))
        gain = gain * jnp.repeat(jnp.exp(steps), extent[dim] // blocks).reshape((-1,) + (1,) * (len(extent) - 1 - dim))
    return gain


def assign_block(own_key, own, number, rows, number_of, top, reach, lean):
    sequence = jax.random.permutation(own_key, number_of)
    heavy_load, ordinary = load_shares(number_of, rows * top, reach, lean, True), load_shares(number_of, rows * top, reach, lean, False)
    places = jnp.arange(number_of)

    def named(tallies, turn):
        used = int((tallies > 0).sum())
        fixed = max(1, used // 4)
        shifted = fixed + (places - fixed + turn * (used - fixed)) % max(1, number_of - fixed)
        return jnp.zeros((number_of,), jnp.int32).at[sequence[jnp.where(places < fixed, places, shifted)]].set(jnp.asarray(tallies, jnp.int32))

    tallies = jnp.where(number % 4 == 0, named(heavy_load, number // 4), named(ordinary, number - number // 4 - 1))
    mixed = jax.random.permutation(jax.random.fold_in(own, 3), number_of)
    donor, receiver = mixed[0:number_of // 2 * 2:2], mixed[1:number_of // 2 * 2:2]
    margin = jnp.minimum(tallies[donor] - 1, reach - tallies[receiver]) // 2
    margin = jnp.where((donor == sequence[0]) | (receiver == sequence[0]) | (tallies[receiver] == 0), 0, jnp.maximum(margin, 0))
    shifted = jax.random.randint(jax.random.fold_in(own, 4), (number_of // 2,), 0, 1 << 20) % (margin + 1)
    tallies = tallies.at[donor].add(-shifted).at[receiver].add(shifted)
    members = jnp.searchsorted(jnp.cumsum(tallies), jnp.arange(rows * top), side="right").astype(jnp.int32)
    table = members.reshape(top, rows).T
    table = table[jax.random.permutation(jax.random.fold_in(own, 1), rows)]
    turn = jax.random.randint(jax.random.fold_in(own, 2), (rows, 1), 0, top)
    return jnp.take_along_axis(table, (jnp.arange(top)[None, :] + turn) % top, axis=1)


def load_shares(amount, total, limit, skew, full):
    weights = [(1 << 20) // math.isqrt(rank ** skew) + 1 for rank in range(1, amount + 1)]
    largest = limit if full else min(limit, max(-(-total // amount), total * weights[0] // sum(weights)))
    least = 1 if total - largest >= amount - 1 else 0
    given, spare = [largest] + [least] * (amount - 1), total - largest - least * (amount - 1)
    while spare > 0:
        free = [i for i in range(1, amount) if given[i] < largest] or [i for i in range(1, amount) if given[i] < limit]
        whole, left = sum([weights[i] for i in free]), spare
        for i in free:
            addition = min(limit - given[i], max(1, left * weights[i] // whole), spare)
            given[i] = given[i] + addition
            spare = spare - addition
    return np.array(given)


def scatter_about(key, dims, scale, limit, split=(), kind=jnp.bfloat16):
    array = scale * jax.random.normal(key, dims, jnp.float32)
    if split:
        array = array * level_of(key, dims, split, -0.22, 0.18)
    return jnp.clip(array, -limit, limit).astype(kind)


def setup_inputs(seed: int = 0) -> dict:
    seeds = jax.random.split(jax.random.key(seed), 11)
    resid = scatter_about(seeds[0], (TOKENS, D), 1.0, 6.0, ((0, 8),))
    mixer_out = scatter_about(seeds[1], (TOKENS, INNER), 1.0, 6.0, ((0, 8), (1, 32)))
    out_proj = scatter_about(seeds[2], (INNER, D), INNER ** -0.5, 0.0625, ((0, 32),))
    norm_gain = jnp.clip(1.0 + 0.18 * jax.random.normal(seeds[3], (D,), jnp.float32), 0.1, 1.9)
    router = scatter_about(seeds[4], (D, EXPERTS), D ** -0.5, 0.09375, (), jnp.float32)
    routes_keys = jax.random.split(jax.random.fold_in(seeds[5], 1), TOKENS // TOK_DEV)
    routes_turns = jax.random.permutation(jax.random.fold_in(seeds[5], 3), TOKENS // TOK_DEV)
    routes = jax.vmap(lambda own, number: assign_block(jax.random.fold_in(seeds[5], 2), own, number, TOK_DEV, EXPERTS, 2, CAP, 2))(routes_keys, routes_turns).reshape((TOKENS, 2))
    w_gate = scatter_about(seeds[6], (2 * EXPERTS, D, FF // 2), D ** -0.5, 0.09375, ((0, 16), (2, 16)))
    w_up = scatter_about(seeds[7], (2 * EXPERTS, D, FF // 2), D ** -0.5, 0.09375, ((0, 16), (2, 16)))
    w_down = scatter_about(seeds[8], (2 * EXPERTS, FF // 2, D), FF ** -0.5, 0.0625, ((0, 16), (1, 16)))
    cotangent = scatter_about(seeds[9], (TOKENS, D), 1.0, 6.0, ((0, 8),))
    return dict(resid=resid, mixer_out=mixer_out, out_proj=out_proj, norm_gain=norm_gain, router=router, routes=routes, w_gate=w_gate, w_up=w_up, w_down=w_down, cotangent=cotangent)


def contract_rows(left, right):
    return lax.dot_general(left, right, (((0,), (0,)), ((), ())), preferred_element_type=jnp.float32)

def contract_cols(left, right):
    return lax.dot_general(left, right, (((1,), (1,)), ((), ())), preferred_element_type=jnp.float32)

def norm_forward(hidden, norm_gain):
    inv_rms = lax.rsqrt(lax.optimization_barrier(jnp.mean(hidden * hidden, axis=1, keepdims=True)) + 1e-05)
    return ((hidden * inv_rms * norm_gain).astype(jnp.bfloat16), inv_rms)

def norm_backward(hidden, inv_rms, norm_gain, normed_cot):
    weighted = normed_cot * norm_gain
    inner_mean = lax.optimization_barrier(jnp.mean(weighted * hidden, axis=1, keepdims=True))
    return inv_rms * weighted - inv_rms * inv_rms * inv_rms * hidden * inner_mean

def pair_slots(pair_expert, expert_count):
    onehot = (pair_expert[:, None] == jnp.arange(expert_count, dtype=jnp.int32)[None, :]).astype(jnp.int32)
    before = jnp.cumsum(onehot, axis=0) - onehot
    return (lax.optimization_barrier(jnp.sum(before * onehot, axis=1)), onehot)

def down_blocks(activated, down_w):
    count = N_DP * N_GROUP
    width = activated.shape[1] // count

    def step(total, block_id):
        left = lax.dynamic_slice_in_dim(activated, block_id * width, width, 1)
        right = lax.dynamic_slice_in_dim(down_w, block_id * width, width, 0)
        term = jnp.dot(left, right, preferred_element_type=jnp.float32).astype(jnp.bfloat16)
        term = lax.optimization_barrier(term)
        return (total + term.astype(jnp.float32), None)
    start = jnp.zeros((activated.shape[0], down_w.shape[1]), jnp.float32)
    total, _unused = lax.scan(step, start, jnp.arange(count, dtype=jnp.int32))
    return total

def input_blocks(d_gate, d_up, gate_w, up_w):
    count = N_DP * N_GROUP
    width = d_gate.shape[1] // count

    def step(total, block_id):
        gate_part = lax.dynamic_slice_in_dim(d_gate, block_id * width, width, 1)
        up_part = lax.dynamic_slice_in_dim(d_up, block_id * width, width, 1)
        gate_cols = lax.dynamic_slice_in_dim(gate_w, block_id * width, width, 1)
        up_cols = lax.dynamic_slice_in_dim(up_w, block_id * width, width, 1)
        term = (contract_cols(gate_part, gate_cols) + contract_cols(up_part, up_cols)).astype(jnp.bfloat16)
        term = lax.optimization_barrier(term)
        return (total + term.astype(jnp.float32), None)
    start = jnp.zeros((d_gate.shape[0], gate_w.shape[0]), jnp.float32)
    total, _unused = lax.scan(step, start, jnp.arange(count, dtype=jnp.int32))
    return total

def expert_forward(inputs, gate_pair, up_pair, down_pair):
    gates, ups, acts, halves = ([], [], [], [])
    for half in range(2):
        pre_gate = jnp.dot(inputs, gate_pair[half], preferred_element_type=jnp.float32)
        pre_up = jnp.dot(inputs, up_pair[half], preferred_element_type=jnp.float32)
        activated = (pre_gate * jax.nn.sigmoid(pre_gate) * pre_up).astype(jnp.bfloat16)
        half_out = down_blocks(activated, down_pair[half]).astype(jnp.bfloat16)
        gates.append(pre_gate)
        ups.append(pre_up)
        acts.append(activated)
        halves.append(half_out)
    produced = (halves[0].astype(jnp.float32) + halves[1].astype(jnp.float32)).astype(jnp.bfloat16)
    return (produced, jnp.stack(gates), jnp.stack(ups), jnp.stack(acts))

def expert_backward(out_cot, pre_gates, pre_ups, gate_pair, up_pair, down_pair):
    halves = []
    for half in range(2):
        pre_gate = pre_gates[half]
        pre_up = pre_ups[half]
        act_cot = contract_cols(out_cot, down_pair[half])
        sig_gate = jax.nn.sigmoid(pre_gate)
        d_gate = (act_cot * pre_up * sig_gate * (1.0 + pre_gate * (1.0 - sig_gate))).astype(jnp.bfloat16)
        d_up = (act_cot * pre_gate * sig_gate).astype(jnp.bfloat16)
        halves.append(input_blocks(d_gate, d_up, gate_pair[half], up_pair[half]).astype(jnp.bfloat16))
    return (halves[0].astype(jnp.float32) + halves[1].astype(jnp.float32)).astype(jnp.bfloat16)

def reference(resid, mixer_out, out_proj, norm_gain, router, routes, w_gate, w_up, w_down, cotangent):
    group_count = N_TENSOR * N_GROUP

    def add_group(running, group_id):
        part_y = lax.dynamic_slice_in_dim(mixer_out, group_id * CH, CH, 1)
        part_w = lax.dynamic_slice_in_dim(out_proj, group_id * CH, CH, 0)
        part_term = jnp.dot(part_y, part_w, preferred_element_type=jnp.float32).astype(jnp.bfloat16)
        part_term = lax.optimization_barrier(part_term)
        return (running + part_term.astype(jnp.float32), None)
    summed, _unused = lax.scan(add_group, jnp.zeros((TOKENS, D), jnp.float32), jnp.arange(group_count, dtype=jnp.int32))
    hidden = resid.astype(jnp.float32) + summed
    normed, inv_rms = norm_forward(hidden, norm_gain)
    logits = jnp.dot(normed.astype(jnp.float32), router, precision=lax.Precision.HIGHEST)
    pair_expert = routes.reshape(-1).astype(jnp.int32)
    block_count = TOKENS // TOK_DEV
    slot_pos, onehot = jax.vmap(pair_slots, in_axes=(0, None))(pair_expert.reshape(block_count, 2 * TOK_DEV), EXPERTS)
    onehot_f = onehot.reshape(2 * TOKENS, EXPERTS).astype(jnp.float32)
    pair_block = jnp.arange(2 * TOKENS, dtype=jnp.int32) // (2 * TOK_DEV)
    position = (pair_block * CAP + slot_pos.reshape(-1)).astype(jnp.int32)
    pair_logit = lax.optimization_barrier(jnp.sum(jnp.repeat(logits, 2, axis=0) * onehot_f, axis=1))
    gate_vals = jax.nn.sigmoid(pair_logit)
    pair_rows = jnp.repeat(normed, 2, axis=0)
    half_units = w_gate.shape[2]
    gate_pairs = w_gate.reshape(EXPERTS, 2, D, half_units)
    up_pairs = w_up.reshape(EXPERTS, 2, D, half_units)
    down_pairs = w_down.reshape(EXPERTS, 2, half_units, D)
    buffer = jnp.zeros((EXPERTS, block_count * CAP, D), jnp.bfloat16).at[pair_expert, position].set(pair_rows)
    produced, pre_gate, pre_up, activated = lax.map(lambda packed: expert_forward(packed[0], packed[1], packed[2], packed[3]), (buffer, gate_pairs, up_pairs, down_pairs))
    pair_out = produced[pair_expert, position]
    mixture = lax.optimization_barrier(jnp.sum((gate_vals[:, None] * pair_out.astype(jnp.float32)).reshape(TOKENS, 2, D), axis=1))
    layer_out = (hidden + mixture).astype(jnp.bfloat16)
    cot_full = cotangent.astype(jnp.float32)
    pair_cot = jnp.repeat(cot_full, 2, axis=0)
    out_cot = (gate_vals[:, None] * pair_cot).astype(jnp.bfloat16)
    gate_cot = lax.optimization_barrier(jnp.sum(pair_cot * pair_out.astype(jnp.float32), axis=1))
    cot_buffer = jnp.zeros((EXPERTS, block_count * CAP, D), jnp.bfloat16).at[pair_expert, position].set(out_cot)
    in_cot = lax.map(lambda packed: expert_backward(packed[0], packed[1], packed[2], packed[3], packed[4], packed[5]), (cot_buffer, pre_gate, pre_up, gate_pairs, up_pairs, down_pairs))
    grad_down = lax.map(lambda packed: jnp.stack([contract_rows(packed[0][0], packed[1]), contract_rows(packed[0][1], packed[1])]), (activated, cot_buffer))
    grad_down = grad_down.reshape(2 * EXPERTS, half_units, D).astype(jnp.bfloat16)
    pair_in = in_cot[pair_expert, position].astype(jnp.float32)
    normed_cot = lax.optimization_barrier(jnp.sum(pair_in.reshape(TOKENS, 2, D), axis=1))
    logit_pair = gate_cot * gate_vals * (1.0 - gate_vals)
    logit_cot = lax.optimization_barrier(jnp.sum((onehot_f * logit_pair[:, None]).reshape(TOKENS, 2, EXPERTS), axis=1))
    normed_cot = normed_cot + jnp.dot(logit_cot, router.T, precision=lax.Precision.HIGHEST)
    hidden_cot = (cot_full + norm_backward(hidden, inv_rms, norm_gain, normed_cot)).astype(jnp.bfloat16)
    grad_mixer = contract_cols(hidden_cot, out_proj).astype(jnp.bfloat16)
    return (layer_out, grad_mixer, grad_down)
```

```python
import jax
import jax.numpy as jnp
from jax import lax
from jax.sharding import Mesh, PartitionSpec as P

BF = jnp.bfloat16
F32 = jnp.float32
CHIPS = ("y", "xh", "half")


def contract_rows(left, right):
    return lax.dot_general(left, right, (((0,), (0,)), ((), ())), preferred_element_type=F32)


def contract_cols(left, right):
    return lax.dot_general(left, right, (((1,), (1,)), ((), ())), preferred_element_type=F32)


def split_three(values):
    high = lax.reduce_precision(values, 8, 7)
    rest = values - high
    mid = lax.reduce_precision(rest, 8, 7)
    low = rest - mid
    return high.astype(BF), mid.astype(BF), low.astype(BF)


def swap_core(value):
    return lax.ppermute(value, "group", [(0, 1), (1, 0)])


def hop(value, size, back):
    pairs = []
    for z in range(size):
        up, down = (z + 1) % size, (z - 1) % size
        if back:
            up, down = down, up
        pairs += [(2 * z, 2 * up), (2 * z + 1, 2 * down + 1)]
    return lax.ppermute(value, ("dp", "group"), pairs)


def exchange(blocks):
    return lax.all_to_all(blocks, CHIPS, 0, 0)


def join_halves(core, mine, other):
    return jnp.where(
        core == 0, jnp.concatenate((mine, other), 1), jnp.concatenate((other, mine), 1)
    )


def gather_features(core, block):
    rows, width = block.shape
    got = exchange(jnp.broadcast_to(block[None], (16, rows, width)))
    other = swap_core(got)
    mine = jnp.transpose(got, (1, 0, 2)).reshape(rows, 16 * width)
    other = jnp.transpose(other, (1, 0, 2)).reshape(rows, 16 * width)
    return join_halves(core, mine, other)


def on_device(
    resid, mixer_out, out_proj, norm_gain, router, routes, w_gate, w_up, w_down, cotangent
):
    rows, width = resid.shape
    experts = router.shape[1]
    units = w_gate.shape[2]
    cap = min(rows, 3 * rows // experts)
    half_width = width // 2
    block = half_width // 16
    z = lax.axis_index("dp")
    core = lax.axis_index("group")
    chip = (lax.axis_index("y") * 2 + lax.axis_index("xh")) * 2 + lax.axis_index("half")
    expert = lax.axis_index("y") * 2 + lax.axis_index("xh")
    first = core * half_width + chip * block

    pair_expert = routes.reshape(-1)
    onehot = (pair_expert[:, None] == jnp.arange(experts, dtype=jnp.int32)[None, :])
    before = jnp.dot(
        (jnp.arange(2 * rows)[:, None] > jnp.arange(2 * rows)[None, :]).astype(BF),
        onehot.astype(BF),
        preferred_element_type=F32,
    )
    slot = jnp.sum(before * onehot.astype(F32), axis=1).astype(jnp.int32)
    target = (pair_expert * cap + slot).reshape(rows, 2)
    own_slots = expert * cap + jnp.arange(cap, dtype=jnp.int32)
    select = (
        (target[None, :, 0] == own_slots[:, None]) | (target[None, :, 1] == own_slots[:, None])
    ).astype(BF)

    own_cots = jnp.dot(select, cotangent, preferred_element_type=F32).astype(BF)
    all_cots = lax.all_gather(own_cots, "dp", axis=0)

    term = jnp.dot(mixer_out, out_proj, preferred_element_type=F32).astype(BF)
    sent = lax.dynamic_slice_in_dim(term, (1 - core) * half_width, half_width, 1)
    kept = lax.dynamic_slice_in_dim(term, core * half_width, half_width, 1)
    chip_term = (kept.astype(F32) + swap_core(sent).astype(F32)).astype(BF)
    blocks = exchange(jnp.transpose(chip_term.reshape(rows, 16, block), (1, 0, 2)))
    hidden = lax.dynamic_slice_in_dim(resid, first, block, 1).astype(F32) + jnp.sum(
        blocks.astype(F32), axis=0
    )
    whole = gather_features(core, hidden.astype(BF)).astype(F32)
    inv_rms = lax.rsqrt(jnp.mean(whole * whole, axis=1, keepdims=True) + 1e-05)
    normed = (whole * inv_rms * norm_gain).astype(BF)
    own_rows = jnp.dot(select, normed, preferred_element_type=F32).astype(BF)

    near = [own_rows]
    for _ in range(3):
        near.append(hop(near[-1], 8, False))
    far = hop(
        lax.dynamic_slice_in_dim(near[3], core * half_width, half_width, 1), 8, False
    )
    others = [swap_core(value) for value in near[1:]]
    far = join_halves(core, far, swap_core(far))
    inputs = jnp.concatenate(near + others + [far], axis=0)
    sign = 1 - 2 * core
    order = [z, z - sign, z - 2 * sign, z - 3 * sign, z + sign, z + 2 * sign, z + 3 * sign, z + 4]
    cots = jnp.concatenate(
        [lax.dynamic_index_in_dim(all_cots, (place + 8) % 8, 0, False) for place in order], axis=0
    )

    own_router = lax.dynamic_index_in_dim(router.T, expert, 0, True)
    r_high, r_mid, r_low = split_three(own_router)
    logit = jnp.sum(
        contract_cols(inputs, jnp.concatenate((r_high, r_mid, r_low), 0)), axis=1, keepdims=True
    )
    gate = jax.nn.sigmoid(logit)
    pre_gate = jnp.dot(inputs, w_gate[0], preferred_element_type=F32)
    pre_up = jnp.dot(inputs, w_up[0], preferred_element_type=F32)
    sig = jax.nn.sigmoid(pre_gate)
    activated = (pre_gate * sig * pre_up).astype(BF)
    out_part = jnp.dot(activated, w_down[0], preferred_element_type=F32).astype(BF)
    out_cot = (gate * cots.astype(F32)).astype(BF)
    act_cot = contract_cols(out_cot, w_down[0])
    d_gate = (act_cot * pre_up * sig * (1.0 + pre_gate * (1.0 - sig))).astype(BF)
    d_up = (act_cot * pre_gate * sig).astype(BF)
    gate_term = (1.0 - gate) * jnp.sum(activated.astype(F32) * act_cot, axis=1, keepdims=True)
    in_part = (
        contract_cols(d_gate, w_gate[0]) + contract_cols(d_up, w_up[0]) + gate_term * own_router
    ).astype(BF)
    grad_down = contract_rows(activated, out_cot).astype(BF)[None]

    def collect(part):
        parts = part.reshape(8, cap, width)
        far_sent = lax.dynamic_slice_in_dim(parts[7], (1 - core) * half_width, half_width, 1)
        far_kept = lax.dynamic_slice_in_dim(parts[7], core * half_width, half_width, 1)
        total = (far_kept.astype(F32) + swap_core(far_sent).astype(F32)).astype(BF)
        total = hop(total, 8, True).astype(F32)
        nothing = jnp.zeros_like(total)
        total = join_halves(core, total, nothing)
        for place in (3, 2, 1):
            total = total + parts[place].astype(F32) + swap_core(parts[place + 3]).astype(F32)
            total = hop(total.astype(BF), 8, True).astype(F32)
        total = (total + parts[0].astype(F32)).astype(BF)
        return total.astype(F32) + swap_core(total).astype(F32)

    half_out = collect(out_part)
    half_in = collect(in_part)

    own_gate = gate[:cap]
    mean_part = jnp.sum(half_in * own_rows.astype(F32), axis=1)
    mean_high = lax.reduce_precision(mean_part, 8, 7)
    mean_low = mean_part - mean_high
    scaled = (own_gate * half_out).astype(BF)
    both = jnp.concatenate((scaled, half_in.astype(BF)), axis=0)
    both = lax.dynamic_slice_in_dim(both, core * half_width, half_width, 1)
    both = jnp.transpose(both.reshape(2 * cap, 16, block), (1, 0, 2))
    means = jnp.concatenate((mean_high, mean_low, jnp.zeros((block - 2 * cap,), F32))).astype(BF)
    message = jnp.concatenate(
        (both, jnp.broadcast_to(means[None, None], (16, 16, block))), axis=1
    )
    got = exchange(message)
    places = jnp.arange(experts * cap, dtype=jnp.int32)
    spread = (
        (target[:, :1] == places[None, :]) | (target[:, 1:] == places[None, :])
    ).reshape(rows, experts, 1, cap)
    spread = jnp.broadcast_to(spread, (rows, experts, 2, cap)).reshape(rows, 16 * cap)
    mixture = jnp.dot(
        spread.astype(BF), got[:, :cap].reshape(16 * cap, block), preferred_element_type=F32
    )
    normed_cot = jnp.dot(
        spread.astype(BF),
        got[:, cap : 2 * cap].reshape(16 * cap, block),
        preferred_element_type=F32,
    )
    means = got[:, 2 * cap, :cap].astype(F32) + got[:, 2 * cap, cap : 2 * cap].astype(F32)
    inner = jnp.sum(spread.astype(F32) * means.reshape(1, 16 * cap), axis=1, keepdims=True)
    gain_here = lax.dynamic_slice_in_dim(norm_gain, first, block, 0)
    cot_here = lax.dynamic_slice_in_dim(cotangent, first, block, 1).astype(F32)
    layer_here = (hidden + mixture).astype(BF)
    cot_out = (
        cot_here
        + inv_rms * (normed_cot * gain_here)
        - inv_rms * inv_rms * hidden * (inner / width)
    ).astype(BF)
    final = gather_features(core, jnp.concatenate((layer_here, cot_out), axis=0))
    layer_out = final[:rows]
    grad_mixer = contract_cols(final[rows:], out_proj).astype(BF)
    return (layer_out, grad_mixer, grad_down)


def solution(mesh):
    fine = Mesh(mesh.devices.reshape(8, 4, 2, 2, 2), ("dp", "y", "xh", "half", "group"))
    tensor = ("y", "xh", "half")
    plane = tensor + ("group",)
    slices = ("dp", "group")
    placed = (
        P("dp", None),
        P("dp", plane),
        P(plane, None),
        P(),
        P(),
        P("dp", None),
        P(tensor, None, slices),
        P(tensor, None, slices),
        P(tensor, slices, None),
        P("dp", None),
    )
    return jax.shard_map(
        on_device,
        mesh=fine,
        in_specs=placed,
        out_specs=(P("dp", None), P("dp", plane), P(tensor, slices, None)),
        check_vma=False,
    )
```

```python
import jax
import jax.numpy as jnp
from jax import lax
from jax.sharding import Mesh, PartitionSpec as P

BF = jnp.bfloat16
F32 = jnp.float32
CHIPS = ("y", "xh", "half")


def contract_rows(left, right):
    return lax.dot_general(left, right, (((0,), (0,)), ((), ())), preferred_element_type=F32)


def contract_cols(left, right):
    return lax.dot_general(left, right, (((1,), (1,)), ((), ())), preferred_element_type=F32)


def split_three(values):
    high = lax.reduce_precision(values, 8, 7)
    rest = values - high
    mid = lax.reduce_precision(rest, 8, 7)
    low = rest - mid
    return high.astype(BF), mid.astype(BF), low.astype(BF)


def swap_core(value):
    return lax.ppermute(value, "group", [(0, 1), (1, 0)])


def hop(value, size, back):
    pairs = []
    for z in range(size):
        up, down = (z + 1) % size, (z - 1) % size
        if back:
            up, down = down, up
        pairs += [(2 * z, 2 * up), (2 * z + 1, 2 * down + 1)]
    return lax.ppermute(value, ("dp", "group"), pairs)


def exchange(blocks):
    return lax.all_to_all(blocks, CHIPS, 0, 0)


def join_halves(core, mine, other):
    return jnp.where(
        core == 0, jnp.concatenate((mine, other), 1), jnp.concatenate((other, mine), 1)
    )


def gather_features(core, block):
    rows, width = block.shape
    got = exchange(jnp.broadcast_to(block[None], (16, rows, width)))
    other = swap_core(got)
    mine = jnp.transpose(got, (1, 0, 2)).reshape(rows, 16 * width)
    other = jnp.transpose(other, (1, 0, 2)).reshape(rows, 16 * width)
    return join_halves(core, mine, other)


def on_device(
    resid, mixer_out, out_proj, norm_gain, router, routes, w_gate, w_up, w_down, cotangent
):
    rows, width = resid.shape
    experts = router.shape[1]
    units = w_gate.shape[2]
    cap = min(rows, 3 * rows // experts)
    half_width = width // 2
    block = half_width // 16
    z = lax.axis_index("dp")
    core = lax.axis_index("group")
    chip = (lax.axis_index("y") * 2 + lax.axis_index("xh")) * 2 + lax.axis_index("half")
    expert = lax.axis_index("y") * 2 + lax.axis_index("xh")
    first = core * half_width + chip * block

    pair_expert = routes.reshape(-1)
    onehot = (pair_expert[:, None] == jnp.arange(experts, dtype=jnp.int32)[None, :])
    before = jnp.dot(
        (jnp.arange(2 * rows)[:, None] > jnp.arange(2 * rows)[None, :]).astype(BF),
        onehot.astype(BF),
        preferred_element_type=F32,
    )
    slot = jnp.sum(before * onehot.astype(F32), axis=1).astype(jnp.int32)
    target = (pair_expert * cap + slot).reshape(rows, 2)
    own_slots = expert * cap + jnp.arange(cap, dtype=jnp.int32)
    select = (
        (target[None, :, 0] == own_slots[:, None]) | (target[None, :, 1] == own_slots[:, None])
    ).astype(BF)

    own_cots = jnp.dot(select, cotangent, preferred_element_type=F32).astype(BF)
    mixer_out, own_cots = lax.optimization_barrier((mixer_out, own_cots))
    all_cots = lax.all_gather(own_cots, "dp", axis=0)
    term = jnp.dot(mixer_out, out_proj, preferred_element_type=F32).astype(BF)
    sent = lax.dynamic_slice_in_dim(term, (1 - core) * half_width, half_width, 1)
    kept = lax.dynamic_slice_in_dim(term, core * half_width, half_width, 1)
    chip_term = (kept.astype(F32) + swap_core(sent).astype(F32)).astype(BF)
    blocks = exchange(jnp.transpose(chip_term.reshape(rows, 16, block), (1, 0, 2)))
    hidden = lax.dynamic_slice_in_dim(resid, first, block, 1).astype(F32) + jnp.sum(
        blocks.astype(F32), axis=0
    )
    whole = gather_features(core, hidden.astype(BF)).astype(F32)
    inv_rms = lax.rsqrt(jnp.mean(whole * whole, axis=1, keepdims=True) + 1e-05)
    normed = (whole * inv_rms * norm_gain).astype(BF)
    own_rows = jnp.dot(select, normed, preferred_element_type=F32).astype(BF)

    own_rows, all_cots = lax.optimization_barrier((own_rows, all_cots))
    near = [own_rows]
    for _ in range(3):
        near.append(hop(near[-1], 8, False))
    far = hop(
        lax.dynamic_slice_in_dim(near[3], core * half_width, half_width, 1), 8, False
    )
    others = [swap_core(value) for value in near[1:]]
    far = join_halves(core, far, swap_core(far))
    inputs = jnp.concatenate(near + others + [far], axis=0)
    sign = 1 - 2 * core
    order = [z, z - sign, z - 2 * sign, z - 3 * sign, z + sign, z + 2 * sign, z + 3 * sign, z + 4]
    cots = jnp.concatenate(
        [lax.dynamic_index_in_dim(all_cots, (place + 8) % 8, 0, False) for place in order], axis=0
    )

    own_router = lax.dynamic_index_in_dim(router.T, expert, 0, True)
    r_high, r_mid, r_low = split_three(own_router)
    logit = jnp.sum(
        contract_cols(inputs, jnp.concatenate((r_high, r_mid, r_low), 0)), axis=1, keepdims=True
    )
    gate = jax.nn.sigmoid(logit)
    pre_gate = jnp.dot(inputs, w_gate[0], preferred_element_type=F32)
    pre_up = jnp.dot(inputs, w_up[0], preferred_element_type=F32)
    sig = jax.nn.sigmoid(pre_gate)
    activated = (pre_gate * sig * pre_up).astype(BF)
    out_part = jnp.dot(activated, w_down[0], preferred_element_type=F32).astype(BF)
    out_cot = (gate * cots.astype(F32)).astype(BF)
    act_cot = contract_cols(out_cot, w_down[0])
    d_gate = (act_cot * pre_up * sig * (1.0 + pre_gate * (1.0 - sig))).astype(BF)
    d_up = (act_cot * pre_gate * sig).astype(BF)
    gate_term = (1.0 - gate) * jnp.sum(activated.astype(F32) * act_cot, axis=1, keepdims=True)
    in_part = (
        contract_cols(d_gate, w_gate[0]) + contract_cols(d_up, w_up[0]) + gate_term * own_router
    ).astype(BF)
    grad_down = contract_rows(activated, out_cot).astype(BF)[None]

    def collect(part):
        parts = part.reshape(8, cap, width)
        far_sent = lax.dynamic_slice_in_dim(parts[7], (1 - core) * half_width, half_width, 1)
        far_kept = lax.dynamic_slice_in_dim(parts[7], core * half_width, half_width, 1)
        total = (far_kept.astype(F32) + swap_core(far_sent).astype(F32)).astype(BF)
        total = hop(total, 8, True).astype(F32)
        nothing = jnp.zeros_like(total)
        total = join_halves(core, total, nothing)
        for place in (3, 2, 1):
            total = total + parts[place].astype(F32) + swap_core(parts[place + 3]).astype(F32)
            total = hop(total.astype(BF), 8, True).astype(F32)
        total = (total + parts[0].astype(F32)).astype(BF)
        return total.astype(F32) + swap_core(total).astype(F32)

    half_out = collect(out_part)
    half_in = collect(in_part)

    own_gate = gate[:cap]
    mean_part = jnp.sum(half_in * own_rows.astype(F32), axis=1)
    mean_high = lax.reduce_precision(mean_part, 8, 7)
    mean_low = mean_part - mean_high
    scaled = (own_gate * half_out).astype(BF)
    both = jnp.concatenate((scaled, half_in.astype(BF)), axis=0)
    both = lax.dynamic_slice_in_dim(both, core * half_width, half_width, 1)
    both = jnp.transpose(both.reshape(2 * cap, 16, block), (1, 0, 2))
    means = jnp.concatenate((mean_high, mean_low, jnp.zeros((block - 2 * cap,), F32))).astype(BF)
    message = jnp.concatenate(
        (both, jnp.broadcast_to(means[None, None], (16, 16, block))), axis=1
    )
    got = exchange(message)
    places = jnp.arange(experts * cap, dtype=jnp.int32)
    spread = (
        (target[:, :1] == places[None, :]) | (target[:, 1:] == places[None, :])
    ).reshape(rows, experts, 1, cap)
    spread = jnp.broadcast_to(spread, (rows, experts, 2, cap)).reshape(rows, 16 * cap)
    mixture = jnp.dot(
        spread.astype(BF), got[:, :cap].reshape(16 * cap, block), preferred_element_type=F32
    )
    normed_cot = jnp.dot(
        spread.astype(BF),
        got[:, cap : 2 * cap].reshape(16 * cap, block),
        preferred_element_type=F32,
    )
    means = got[:, 2 * cap, :cap].astype(F32) + got[:, 2 * cap, cap : 2 * cap].astype(F32)
    inner = jnp.sum(spread.astype(F32) * means.reshape(1, 16 * cap), axis=1, keepdims=True)
    gain_here = lax.dynamic_slice_in_dim(norm_gain, first, block, 0)
    cot_here = lax.dynamic_slice_in_dim(cotangent, first, block, 1).astype(F32)
    layer_here = (hidden + mixture).astype(BF)
    cot_out = (
        cot_here
        + inv_rms * (normed_cot * gain_here)
        - inv_rms * inv_rms * hidden * (inner / width)
    ).astype(BF)
    final = gather_features(core, jnp.concatenate((layer_here, cot_out), axis=0))
    layer_out = final[:rows]
    grad_mixer = contract_cols(final[rows:], out_proj).astype(BF)
    return (layer_out, grad_mixer, grad_down)


def solution(mesh):
    fine = Mesh(mesh.devices.reshape(8, 4, 2, 2, 2), ("dp", "y", "xh", "half", "group"))
    tensor = ("y", "xh", "half")
    plane = tensor + ("group",)
    slices = ("dp", "group")
    placed = (
        P("dp", None),
        P("dp", plane),
        P(plane, None),
        P(),
        P(),
        P("dp", None),
        P(tensor, None, slices),
        P(tensor, None, slices),
        P(tensor, slices, None),
        P("dp", None),
    )
    return jax.shard_map(
        on_device,
        mesh=fine,
        in_specs=placed,
        out_specs=(P("dp", None), P("dp", plane), P(tensor, slices, None)),
        check_vma=False,
    )
```

```python
import jax
import jax.numpy as jnp
from jax import lax
from jax.experimental import pallas as pl
from jax.experimental.pallas import tpu as pltpu
from jax.sharding import Mesh, PartitionSpec as P

BF = jnp.bfloat16
F32 = jnp.float32
CHIPS = ("y", "xh", "half")


def contract_rows(left, right):
    return lax.dot_general(left, right, (((0,), (0,)), ((), ())), preferred_element_type=F32)


def contract_cols(left, right):
    return lax.dot_general(left, right, (((1,), (1,)), ((), ())), preferred_element_type=F32)


def split_three(values):
    high = lax.reduce_precision(values, 8, 7)
    rest = values - high
    mid = lax.reduce_precision(rest, 8, 7)
    low = rest - mid
    return high.astype(BF), mid.astype(BF), low.astype(BF)


def swap_core(value):
    return lax.ppermute(value, "group", [(0, 1), (1, 0)])


def hop(value, size, step):
    return lax.ppermute(value, "dp", [(z, (z + step) % size) for z in range(size)])


def exchange(blocks):
    return lax.all_to_all(blocks, CHIPS, 0, 0)


def join_halves(core, mine, other):
    return jnp.where(
        core == 0, jnp.concatenate((mine, other), 1), jnp.concatenate((other, mine), 1)
    )


def gather_half(block):
    rows, width = block.shape
    got = exchange(jnp.broadcast_to(block[None], (16, rows, width)))
    return got


def flat(blocks):
    return jnp.transpose(blocks, (1, 0, 2)).reshape(blocks.shape[1], -1)


def finish_kernel(core_ref, mine_ref, other_ref, proj_ref, layer_ref, grad_ref, cot_ref):
    rows, width = layer_ref.shape
    block = mine_ref.shape[2]
    core = core_ref[0]
    for chip in range(16):
        for ref, number in ((mine_ref, core), (other_ref, 1 - core)):
            start = pl.multiple_of(number * (width // 2) + chip * block, block)
            layer_ref[:, pl.ds(start, block)] = ref[chip, :rows]
            cot_ref[:, pl.ds(start, block)] = ref[chip, rows:]
    grad_ref[...] = contract_cols(cot_ref[...], proj_ref[...]).astype(BF)


def finish(core, mine, other, out_proj):
    rows = mine.shape[1] // 2
    channels, width = out_proj.shape
    vmem = pl.BlockSpec(memory_space=pltpu.VMEM)
    return pl.pallas_call(
        finish_kernel,
        out_shape=(
            jax.ShapeDtypeStruct((rows, width), BF),
            jax.ShapeDtypeStruct((rows, channels), BF),
        ),
        in_specs=[pl.BlockSpec(memory_space=pltpu.SMEM), vmem, vmem, vmem],
        out_specs=(vmem, vmem),
        scratch_shapes=[pltpu.VMEM((rows, width), BF)],
        compiler_params=pltpu.CompilerParams(vmem_limit_bytes=32 * 1024 * 1024),
    )(core.reshape(1), mine, other, out_proj)


def on_device(
    resid, mixer_out, out_proj, norm_gain, router, routes, w_gate, w_up, w_down, cotangent
):
    rows, width = resid.shape
    experts = router.shape[1]
    units = w_gate.shape[2]
    cap = min(rows, 3 * rows // experts)
    half_width = width // 2
    block = half_width // 16
    z = lax.axis_index("dp")
    core = lax.axis_index("group")
    chip = (lax.axis_index("y") * 2 + lax.axis_index("xh")) * 2 + lax.axis_index("half")
    expert = lax.axis_index("y") * 2 + lax.axis_index("xh")
    first = core * half_width + chip * block

    pair_expert = routes.reshape(-1)
    onehot = (pair_expert[:, None] == jnp.arange(experts, dtype=jnp.int32)[None, :])
    before = jnp.dot(
        (jnp.arange(2 * rows)[:, None] > jnp.arange(2 * rows)[None, :]).astype(BF),
        onehot.astype(BF),
        preferred_element_type=F32,
    )
    slot = jnp.sum(before * onehot.astype(F32), axis=1).astype(jnp.int32)
    target = (pair_expert * cap + slot).reshape(rows, 2)
    own_slots = expert * cap + jnp.arange(cap, dtype=jnp.int32)
    select = (
        (target[None, :, 0] == own_slots[:, None]) | (target[None, :, 1] == own_slots[:, None])
    ).astype(BF)

    cot_half = lax.dynamic_slice_in_dim(cotangent, core * half_width, half_width, 1)
    own_cots = jnp.dot(select, cot_half, preferred_element_type=F32).astype(BF)
    mixer_out, own_cots = lax.optimization_barrier((mixer_out, own_cots))
    all_cots = lax.all_gather(own_cots, ("dp", "group"), axis=0).reshape(8, 2, cap, half_width)

    term = jnp.dot(mixer_out, out_proj, preferred_element_type=F32).astype(BF)
    sent = lax.dynamic_slice_in_dim(term, (1 - core) * half_width, half_width, 1)
    kept = lax.dynamic_slice_in_dim(term, core * half_width, half_width, 1)
    chip_term = (kept.astype(F32) + swap_core(sent).astype(F32)).astype(BF)
    blocks = exchange(jnp.transpose(chip_term.reshape(rows, 16, block), (1, 0, 2)))
    hidden = lax.dynamic_slice_in_dim(resid, first, block, 1).astype(F32) + jnp.sum(
        blocks.astype(F32), axis=0
    )
    whole = flat(gather_half(hidden.astype(BF))).astype(F32)
    squares = jnp.sum(whole * whole, axis=1, keepdims=True)
    squares = jnp.broadcast_to(squares, (rows, 128))
    squares = (squares + swap_core(squares))[:, :1]
    inv_rms = lax.rsqrt(squares / width + 1e-05)
    gain_half = lax.dynamic_slice_in_dim(norm_gain, core * half_width, half_width, 0)
    normed = (whole * inv_rms * gain_half).astype(BF)
    own_rows = jnp.dot(select, normed, preferred_element_type=F32).astype(BF)

    def half_of(value, number, dim):
        return lax.dynamic_slice_in_dim(value, number * half_width, half_width, dim)

    def weights(value, dim):
        return half_of(value, core, dim), swap_core(half_of(value, 1 - core, dim))

    gate_here, gate_there = weights(w_gate[0], 0)
    up_here, up_there = weights(w_up[0], 0)
    down_here, down_there = weights(w_down[0], 1)

    own_rows, all_cots = lax.optimization_barrier((own_rows, all_cots))
    quarter = half_width // 2
    came_up, came_down = [own_rows], [own_rows]
    for _ in range(3):
        came_up.append(hop(came_up[-1], 8, 1))
        came_down.append(hop(came_down[-1], 8, -1))
    far_up = hop(came_up[3][:, :quarter], 8, 1)
    far_down = hop(came_down[3][:, quarter:], 8, -1)
    mine = [own_rows]
    for near in (1, 2, 3):
        mine += [came_up[near], came_down[near]]
    other = [swap_core(value) for value in mine]
    mine.append(jnp.concatenate((far_up, far_down), axis=1))
    other.append(jnp.concatenate((swap_core(far_up), swap_core(far_down)), axis=1))
    inputs = join_halves(core, jnp.concatenate(mine, axis=0), jnp.concatenate(other, axis=0))
    order = [z, z - 1, z + 1, z - 2, z + 2, z - 3, z + 3, z + 4]
    cots = [lax.dynamic_index_in_dim(all_cots, (place + 8) % 8, 0, False) for place in order]
    cots = jnp.concatenate(
        [jnp.concatenate((value[0], value[1]), axis=1) for value in cots], axis=0
    )

    own_router = lax.dynamic_index_in_dim(router.T, expert, 0, True)
    r_high, r_mid, r_low = split_three(own_router)
    logit = jnp.sum(
        contract_cols(inputs, jnp.concatenate((r_high, r_mid, r_low), 0)), axis=1, keepdims=True
    )
    gate = jax.nn.sigmoid(logit)
    pre_gate = jnp.dot(inputs, w_gate[0], preferred_element_type=F32)
    pre_up = jnp.dot(inputs, w_up[0], preferred_element_type=F32)
    sig = jax.nn.sigmoid(pre_gate)
    activated = (pre_gate * sig * pre_up).astype(BF)
    out_part = jnp.dot(activated, down_here, preferred_element_type=F32) + jnp.dot(
        swap_core(activated), down_there, preferred_element_type=F32
    )
    out_cot = (gate * cots.astype(F32)).astype(BF)
    act_cot = contract_cols(out_cot, w_down[0])
    d_gate = (act_cot * pre_up * sig * (1.0 + pre_gate * (1.0 - sig))).astype(BF)
    d_up = (act_cot * pre_gate * sig).astype(BF)
    d_gate_there = swap_core(d_gate)
    d_up_there = swap_core(d_up)
    gate_cot = jnp.sum(activated.astype(F32) * act_cot, axis=1, keepdims=True)
    gate_cot = jnp.broadcast_to(gate_cot, (8 * cap, 128))
    gate_cot = (gate_cot + swap_core(gate_cot))[:, :1]
    in_part = (
        contract_cols(d_gate, gate_here)
        + contract_cols(d_up, up_here)
        + contract_cols(d_gate_there, gate_there)
        + contract_cols(d_up_there, up_there)
        + ((1.0 - gate) * gate_cot) * half_of(own_router, core, 1)
    )
    out_part = out_part.astype(BF).reshape(8, cap, half_width)
    in_part = in_part.astype(BF).reshape(8, cap, half_width)

    def collect(parts, beside):
        down = hop(parts[7, :, :quarter], 8, -1).astype(F32)
        up = hop(parts[7, :, quarter:], 8, 1).astype(F32)
        nothing = jnp.zeros_like(up)
        down = jnp.concatenate((down, nothing), axis=1)
        up = jnp.concatenate((nothing, up), axis=1)
        for near in (3, 2, 1):
            down = hop((down + parts[2 * near - 1].astype(F32)).astype(BF), 8, -1)
            up = hop((up + parts[2 * near].astype(F32)).astype(BF), 8, 1)
            if near == 3 and beside is not None:
                up, beside = lax.optimization_barrier((up, beside))
            down, up = down.astype(F32), up.astype(F32)
        return parts[0].astype(F32) + down + up, beside

    half_out, late = collect(out_part, activated)
    half_in, _ = collect(in_part, None)
    grad_down = contract_rows(late, out_cot).astype(BF)[None]
    half_in, grad_down = lax.optimization_barrier((half_in, grad_down))

    own_gate = gate[:cap]
    mean_part = jnp.sum(half_in * own_rows.astype(F32), axis=1, keepdims=True)
    mean_part = jnp.broadcast_to(mean_part, (cap, 128))
    mean_part = (mean_part + swap_core(mean_part))[:, 0]
    mean_high = lax.reduce_precision(mean_part, 8, 7)
    mean_low = mean_part - mean_high
    scaled = (own_gate * half_out).astype(BF)
    both = jnp.concatenate((scaled, half_in.astype(BF)), axis=0)
    both = jnp.transpose(both.reshape(2 * cap, 16, block), (1, 0, 2))
    means = jnp.concatenate((mean_high, mean_low, jnp.zeros((block - 2 * cap,), F32))).astype(BF)
    message = jnp.concatenate(
        (both, jnp.broadcast_to(means[None, None], (16, 16, block))), axis=1
    )
    got = exchange(message)
    places = jnp.arange(experts * cap, dtype=jnp.int32)
    spread = (
        (target[:, :1] == places[None, :]) | (target[:, 1:] == places[None, :])
    ).reshape(rows, experts, 1, cap)
    spread = jnp.broadcast_to(spread, (rows, experts, 2, cap)).reshape(rows, 16 * cap)
    mixture = jnp.dot(
        spread.astype(BF), got[:, :cap].reshape(16 * cap, block), preferred_element_type=F32
    )
    normed_cot = jnp.dot(
        spread.astype(BF),
        got[:, cap : 2 * cap].reshape(16 * cap, block),
        preferred_element_type=F32,
    )
    means = got[:, 2 * cap, :cap].astype(F32) + got[:, 2 * cap, cap : 2 * cap].astype(F32)
    inner = jnp.sum(spread.astype(F32) * means.reshape(1, 16 * cap), axis=1, keepdims=True)
    gain_here = lax.dynamic_slice_in_dim(norm_gain, first, block, 0)
    cot_here = lax.dynamic_slice_in_dim(cotangent, first, block, 1).astype(F32)
    layer_here = (hidden + mixture).astype(BF)
    cot_out = (
        cot_here
        + inv_rms * (normed_cot * gain_here)
        - inv_rms * inv_rms * hidden * (inner / width)
    ).astype(BF)
    got = gather_half(jnp.concatenate((layer_here, cot_out), axis=0))
    other = swap_core(got)
    layer_out, grad_mixer = finish(core, got, other, out_proj)
    return (layer_out, grad_mixer, grad_down)


def solution(mesh):
    fine = Mesh(mesh.devices.reshape(8, 4, 2, 2, 2), ("dp", "y", "xh", "half", "group"))
    tensor = ("y", "xh", "half")
    plane = tensor + ("group",)
    slices = ("dp", "group")
    placed = (
        P("dp", None),
        P("dp", plane),
        P(plane, None),
        P(),
        P(),
        P("dp", None),
        P(tensor, None, slices),
        P(tensor, None, slices),
        P(tensor, slices, None),
        P("dp", None),
    )
    return jax.shard_map(
        on_device,
        mesh=fine,
        in_specs=placed,
        out_specs=(P("dp", None), P("dp", plane), P(tensor, slices, None)),
        check_vma=False,
    )
```

```python
import jax
import jax.numpy as jnp
from jax import lax
from jax.sharding import Mesh, PartitionSpec as P

BF = jnp.bfloat16
F32 = jnp.float32
CHIPS = ("y", "xh", "half")


def contract_rows(left, right):
    return lax.dot_general(left, right, (((0,), (0,)), ((), ())), preferred_element_type=F32)


def contract_cols(left, right):
    return lax.dot_general(left, right, (((1,), (1,)), ((), ())), preferred_element_type=F32)


def split_three(values):
    high = lax.reduce_precision(values, 8, 7)
    rest = values - high
    mid = lax.reduce_precision(rest, 8, 7)
    low = rest - mid
    return high.astype(BF), mid.astype(BF), low.astype(BF)


def swap_core(value):
    return lax.ppermute(value, "group", [(0, 1), (1, 0)])


def hop(value, size, step):
    return lax.ppermute(value, "dp", [(z, (z + step) % size) for z in range(size)])


def exchange(blocks):
    return lax.all_to_all(blocks, CHIPS, 0, 0)


def join_halves(core, mine, other):
    return jnp.where(
        core == 0, jnp.concatenate((mine, other), 1), jnp.concatenate((other, mine), 1)
    )


def gather_half(block):
    rows, width = block.shape
    got = exchange(jnp.broadcast_to(block[None], (16, rows, width)))
    return got


def flat(blocks):
    return jnp.transpose(blocks, (1, 0, 2)).reshape(blocks.shape[1], -1)


def on_device(
    resid, mixer_out, out_proj, norm_gain, router, routes, w_gate, w_up, w_down, cotangent
):
    rows, width = resid.shape
    experts = router.shape[1]
    units = w_gate.shape[2]
    cap = min(rows, 3 * rows // experts)
    half_width = width // 2
    block = half_width // 16
    z = lax.axis_index("dp")
    core = lax.axis_index("group")
    chip = (lax.axis_index("y") * 2 + lax.axis_index("xh")) * 2 + lax.axis_index("half")
    expert = lax.axis_index("y") * 2 + lax.axis_index("xh")
    first = core * half_width + chip * block

    pair_expert = routes.reshape(-1)
    onehot = (pair_expert[:, None] == jnp.arange(experts, dtype=jnp.int32)[None, :])
    before = jnp.dot(
        (jnp.arange(2 * rows)[:, None] > jnp.arange(2 * rows)[None, :]).astype(BF),
        onehot.astype(BF),
        preferred_element_type=F32,
    )
    slot = jnp.sum(before * onehot.astype(F32), axis=1).astype(jnp.int32)
    target = (pair_expert * cap + slot).reshape(rows, 2)
    own_slots = expert * cap + jnp.arange(cap, dtype=jnp.int32)
    select = (
        (target[None, :, 0] == own_slots[:, None]) | (target[None, :, 1] == own_slots[:, None])
    ).astype(BF)

    cot_half = lax.dynamic_slice_in_dim(cotangent, core * half_width, half_width, 1)
    own_cots = jnp.dot(select, cot_half, preferred_element_type=F32).astype(BF)
    mixer_out, own_cots = lax.optimization_barrier((mixer_out, own_cots))
    all_cots = lax.all_gather(own_cots, ("dp", "group"), axis=0).reshape(8, 2, cap, half_width)

    term = jnp.dot(mixer_out, out_proj, preferred_element_type=F32).astype(BF)
    sent = lax.dynamic_slice_in_dim(term, (1 - core) * half_width, half_width, 1)
    kept = lax.dynamic_slice_in_dim(term, core * half_width, half_width, 1)
    chip_term = (kept.astype(F32) + swap_core(sent).astype(F32)).astype(BF)
    blocks = exchange(jnp.transpose(chip_term.reshape(rows, 16, block), (1, 0, 2)))
    hidden = lax.dynamic_slice_in_dim(resid, first, block, 1).astype(F32) + jnp.sum(
        blocks.astype(F32), axis=0
    )
    whole = flat(gather_half(hidden.astype(BF))).astype(F32)
    squares = jnp.sum(whole * whole, axis=1, keepdims=True)
    squares = jnp.broadcast_to(squares, (rows, 128))
    squares = (squares + swap_core(squares))[:, :1]
    inv_rms = lax.rsqrt(squares / width + 1e-05)
    gain_half = lax.dynamic_slice_in_dim(norm_gain, core * half_width, half_width, 0)
    normed = (whole * inv_rms * gain_half).astype(BF)
    own_rows = jnp.dot(select, normed, preferred_element_type=F32).astype(BF)

    def half_of(value, number, dim):
        return lax.dynamic_slice_in_dim(value, number * half_width, half_width, dim)

    def weights(value, dim):
        return half_of(value, core, dim), swap_core(half_of(value, 1 - core, dim))

    gate_here, gate_there = weights(w_gate[0], 0)
    up_here, up_there = weights(w_up[0], 0)
    down_here, down_there = weights(w_down[0], 1)

    own_rows, all_cots = lax.optimization_barrier((own_rows, all_cots))
    quarter = half_width // 2
    came_up, came_down = [own_rows], [own_rows]
    for _ in range(3):
        came_up.append(hop(came_up[-1], 8, 1))
        came_down.append(hop(came_down[-1], 8, -1))
    far_up = hop(came_up[3][:, :quarter], 8, 1)
    far_down = hop(came_down[3][:, quarter:], 8, -1)
    mine = [own_rows]
    for near in (1, 2, 3):
        mine += [came_up[near], came_down[near]]
    other = [swap_core(value) for value in mine]
    mine.append(jnp.concatenate((far_up, far_down), axis=1))
    other.append(jnp.concatenate((swap_core(far_up), swap_core(far_down)), axis=1))
    inputs = join_halves(core, jnp.concatenate(mine, axis=0), jnp.concatenate(other, axis=0))
    order = [z, z - 1, z + 1, z - 2, z + 2, z - 3, z + 3, z + 4]
    cots = [lax.dynamic_index_in_dim(all_cots, (place + 8) % 8, 0, False) for place in order]
    cots = jnp.concatenate(
        [jnp.concatenate((value[0], value[1]), axis=1) for value in cots], axis=0
    )

    own_router = lax.dynamic_index_in_dim(router.T, expert, 0, True)
    r_high, r_mid, r_low = split_three(own_router)
    logit = jnp.sum(
        contract_cols(inputs, jnp.concatenate((r_high, r_mid, r_low), 0)), axis=1, keepdims=True
    )
    gate = jax.nn.sigmoid(logit)
    pre_gate = jnp.dot(inputs, w_gate[0], preferred_element_type=F32)
    pre_up = jnp.dot(inputs, w_up[0], preferred_element_type=F32)
    sig = jax.nn.sigmoid(pre_gate)
    activated = (pre_gate * sig * pre_up).astype(BF)
    out_part = jnp.dot(activated, down_here, preferred_element_type=F32) + jnp.dot(
        swap_core(activated), down_there, preferred_element_type=F32
    )
    out_cot = (gate * cots.astype(F32)).astype(BF)
    act_cot = contract_cols(out_cot, w_down[0])
    d_gate = (act_cot * pre_up * sig * (1.0 + pre_gate * (1.0 - sig))).astype(BF)
    d_up = (act_cot * pre_gate * sig).astype(BF)
    d_gate_there = swap_core(d_gate)
    d_up_there = swap_core(d_up)
    gate_cot = jnp.sum(activated.astype(F32) * act_cot, axis=1, keepdims=True)
    gate_cot = jnp.broadcast_to(gate_cot, (8 * cap, 128))
    gate_cot = (gate_cot + swap_core(gate_cot))[:, :1]
    in_part = (
        contract_cols(d_gate, gate_here)
        + contract_cols(d_up, up_here)
        + contract_cols(d_gate_there, gate_there)
        + contract_cols(d_up_there, up_there)
        + ((1.0 - gate) * gate_cot) * half_of(own_router, core, 1)
    )
    out_part = out_part.astype(BF).reshape(8, cap, half_width)
    in_part = in_part.astype(BF).reshape(8, cap, half_width)

    def collect(parts, beside):
        down = hop(parts[7, :, :quarter], 8, -1).astype(F32)
        up = hop(parts[7, :, quarter:], 8, 1).astype(F32)
        nothing = jnp.zeros_like(up)
        down = jnp.concatenate((down, nothing), axis=1)
        up = jnp.concatenate((nothing, up), axis=1)
        for near in (3, 2, 1):
            down = hop((down + parts[2 * near - 1].astype(F32)).astype(BF), 8, -1)
            up = hop((up + parts[2 * near].astype(F32)).astype(BF), 8, 1)
            if near == 3 and beside is not None:
                up, beside = lax.optimization_barrier((up, beside))
            down, up = down.astype(F32), up.astype(F32)
        return parts[0].astype(F32) + down + up, beside

    half_out, late = collect(out_part, activated)
    half_in, _ = collect(in_part, None)
    grad_down = contract_rows(late, out_cot).astype(BF)[None]
    half_in, grad_down = lax.optimization_barrier((half_in, grad_down))

    own_gate = gate[:cap]
    mean_part = jnp.sum(half_in * own_rows.astype(F32), axis=1, keepdims=True)
    mean_part = jnp.broadcast_to(mean_part, (cap, 128))
    mean_part = (mean_part + swap_core(mean_part))[:, 0]
    mean_high = lax.reduce_precision(mean_part, 8, 7)
    mean_low = mean_part - mean_high
    scaled = (own_gate * half_out).astype(BF)
    both = jnp.concatenate((scaled, half_in.astype(BF)), axis=0)
    both = jnp.transpose(both.reshape(2 * cap, 16, block), (1, 0, 2))
    means = jnp.concatenate((mean_high, mean_low, jnp.zeros((block - 2 * cap,), F32))).astype(BF)
    message = jnp.concatenate(
        (both, jnp.broadcast_to(means[None, None], (16, 16, block))), axis=1
    )
    got = exchange(message)
    places = jnp.arange(experts * cap, dtype=jnp.int32)
    spread = (
        (target[:, :1] == places[None, :]) | (target[:, 1:] == places[None, :])
    ).reshape(rows, experts, 1, cap)
    spread = jnp.broadcast_to(spread, (rows, experts, 2, cap)).reshape(rows, 16 * cap)
    mixture = jnp.dot(
        spread.astype(BF), got[:, :cap].reshape(16 * cap, block), preferred_element_type=F32
    )
    normed_cot = jnp.dot(
        spread.astype(BF),
        got[:, cap : 2 * cap].reshape(16 * cap, block),
        preferred_element_type=F32,
    )
    means = got[:, 2 * cap, :cap].astype(F32) + got[:, 2 * cap, cap : 2 * cap].astype(F32)
    inner = jnp.sum(spread.astype(F32) * means.reshape(1, 16 * cap), axis=1, keepdims=True)
    gain_here = lax.dynamic_slice_in_dim(norm_gain, first, block, 0)
    cot_here = lax.dynamic_slice_in_dim(cotangent, first, block, 1).astype(F32)
    layer_here = (hidden + mixture).astype(BF)
    cot_out = (
        cot_here
        + inv_rms * (normed_cot * gain_here)
        - inv_rms * inv_rms * hidden * (inner / width)
    ).astype(BF)
    got = gather_half(jnp.concatenate((layer_here, cot_out), axis=0))
    other = swap_core(got)
    layer_out = join_halves(core, flat(got[:, :rows]), flat(other[:, :rows]))
    grad_mixer = (
        contract_cols(flat(got[:, rows:]), half_of(out_proj, core, 1))
        + contract_cols(flat(other[:, rows:]), half_of(out_proj, 1 - core, 1))
    ).astype(BF)
    return (layer_out, grad_mixer, grad_down)


def solution(mesh):
    fine = Mesh(mesh.devices.reshape(8, 4, 2, 2, 2), ("dp", "y", "xh", "half", "group"))
    tensor = ("y", "xh", "half")
    plane = tensor + ("group",)
    slices = ("dp", "group")
    placed = (
        P("dp", None),
        P("dp", plane),
        P(plane, None),
        P(),
        P(),
        P("dp", None),
        P(tensor, None, slices),
        P(tensor, None, slices),
        P(tensor, slices, None),
        P("dp", None),
    )
    return jax.shard_map(
        on_device,
        mesh=fine,
        in_specs=placed,
        out_specs=(P("dp", None), P("dp", plane), P(tensor, slices, None)),
        check_vma=False,
    )
```

```python
import jax
import jax.numpy as jnp
from jax import lax
from jax.experimental import pallas as pl
from jax.experimental.pallas import tpu as pltpu
from jax.sharding import Mesh, PartitionSpec as P

BF = jnp.bfloat16
F32 = jnp.float32
CHIPS = ("y", "xh", "half")


def contract_rows(left, right):
    return lax.dot_general(left, right, (((0,), (0,)), ((), ())), preferred_element_type=F32)


def contract_cols(left, right):
    return lax.dot_general(left, right, (((1,), (1,)), ((), ())), preferred_element_type=F32)


def split_three(values):
    high = lax.reduce_precision(values, 8, 7)
    rest = values - high
    mid = lax.reduce_precision(rest, 8, 7)
    low = rest - mid
    return high.astype(BF), mid.astype(BF), low.astype(BF)


def swap_core(value):
    return lax.ppermute(value, "group", [(0, 1), (1, 0)])


def hop(value, size, back):
    pairs = []
    for z in range(size):
        up, down = (z + 1) % size, (z - 1) % size
        if back:
            up, down = down, up
        pairs += [(2 * z, 2 * up), (2 * z + 1, 2 * down + 1)]
    return lax.ppermute(value, ("dp", "group"), pairs)


def exchange(blocks):
    return lax.all_to_all(blocks, CHIPS, 0, 0)


def join_halves(core, mine, other):
    return jnp.where(
        core == 0, jnp.concatenate((mine, other), 1), jnp.concatenate((other, mine), 1)
    )


def gather_features(core, block):
    rows, width = block.shape
    got = exchange(jnp.broadcast_to(block[None], (16, rows, width)))
    other = swap_core(got)
    mine = jnp.transpose(got, (1, 0, 2)).reshape(rows, 16 * width)
    other = jnp.transpose(other, (1, 0, 2)).reshape(rows, 16 * width)
    return join_halves(core, mine, other)


def finish_kernel(core_ref, mine_ref, other_ref, proj_ref, layer_ref, grad_ref, cot_ref, total_ref):
    rows, width = layer_ref.shape
    block = mine_ref.shape[2]
    core = core_ref[0]
    half = width // 2

    def place(chip, carry):
        for ref, number in ((mine_ref, core), (other_ref, 1 - core)):
            start = pl.multiple_of(number * half + chip * block, block)
            layer_ref[:, pl.ds(start, block)] = ref[chip, :rows]
            cot_ref[:, pl.ds(start, block)] = ref[chip, rows:]
        return carry

    lax.fori_loop(0, 16, place, 0)
    total_ref[...] = jnp.zeros_like(total_ref)

    def multiply(part, carry):
        columns = pl.ds(pl.multiple_of(part * 1024, 1024), 1024)
        total_ref[...] += contract_cols(cot_ref[:, columns], proj_ref[:, columns])
        return carry

    lax.fori_loop(0, width // 1024, multiply, 0)
    grad_ref[...] = total_ref[...].astype(BF)


def finish(core, mine, other, out_proj):
    rows = mine.shape[1] // 2
    channels, width = out_proj.shape
    vmem = pl.BlockSpec(memory_space=pltpu.VMEM)
    return pl.pallas_call(
        finish_kernel,
        out_shape=(
            jax.ShapeDtypeStruct((rows, width), BF),
            jax.ShapeDtypeStruct((rows, channels), BF),
        ),
        in_specs=[pl.BlockSpec(memory_space=pltpu.SMEM), vmem, vmem, vmem],
        out_specs=(vmem, vmem),
        scratch_shapes=[pltpu.VMEM((rows, width), BF), pltpu.VMEM((rows, channels), F32)],
        compiler_params=pltpu.CompilerParams(vmem_limit_bytes=32 * 1024 * 1024),
    )(core.reshape(1), mine, other, out_proj)


def on_device(
    resid, mixer_out, out_proj, norm_gain, router, routes, w_gate, w_up, w_down, cotangent
):
    rows, width = resid.shape
    experts = router.shape[1]
    units = w_gate.shape[2]
    cap = min(rows, 3 * rows // experts)
    half_width = width // 2
    block = half_width // 16
    z = lax.axis_index("dp")
    core = lax.axis_index("group")
    chip = (lax.axis_index("y") * 2 + lax.axis_index("xh")) * 2 + lax.axis_index("half")
    expert = lax.axis_index("y") * 2 + lax.axis_index("xh")
    first = core * half_width + chip * block

    pair_expert = routes.reshape(-1)
    onehot = (pair_expert[:, None] == jnp.arange(experts, dtype=jnp.int32)[None, :])
    before = jnp.dot(
        (jnp.arange(2 * rows)[:, None] > jnp.arange(2 * rows)[None, :]).astype(BF),
        onehot.astype(BF),
        preferred_element_type=F32,
    )
    slot = jnp.sum(before * onehot.astype(F32), axis=1).astype(jnp.int32)
    target = (pair_expert * cap + slot).reshape(rows, 2)
    own_slots = expert * cap + jnp.arange(cap, dtype=jnp.int32)
    select = (
        (target[None, :, 0] == own_slots[:, None]) | (target[None, :, 1] == own_slots[:, None])
    ).astype(BF)

    own_cots = jnp.dot(select, cotangent, preferred_element_type=F32).astype(BF)
    mixer_out, own_cots = lax.optimization_barrier((mixer_out, own_cots))
    all_cots = lax.all_gather(own_cots, "dp", axis=0)
    term = jnp.dot(mixer_out, out_proj, preferred_element_type=F32).astype(BF)
    sent = lax.dynamic_slice_in_dim(term, (1 - core) * half_width, half_width, 1)
    kept = lax.dynamic_slice_in_dim(term, core * half_width, half_width, 1)
    chip_term = (kept.astype(F32) + swap_core(sent).astype(F32)).astype(BF)
    blocks = exchange(jnp.transpose(chip_term.reshape(rows, 16, block), (1, 0, 2)))
    hidden = lax.dynamic_slice_in_dim(resid, first, block, 1).astype(F32) + jnp.sum(
        blocks.astype(F32), axis=0
    )
    whole = gather_features(core, hidden.astype(BF)).astype(F32)
    inv_rms = lax.rsqrt(jnp.mean(whole * whole, axis=1, keepdims=True) + 1e-05)
    normed = (whole * inv_rms * norm_gain).astype(BF)
    own_rows = jnp.dot(select, normed, preferred_element_type=F32).astype(BF)

    own_rows, all_cots = lax.optimization_barrier((own_rows, all_cots))
    near = [own_rows]
    for _ in range(3):
        near.append(hop(near[-1], 8, False))
    far = hop(
        lax.dynamic_slice_in_dim(near[3], core * half_width, half_width, 1), 8, False
    )
    others = [swap_core(value) for value in near[1:]]
    far = join_halves(core, far, swap_core(far))
    inputs = jnp.concatenate(near + others + [far], axis=0)
    sign = 1 - 2 * core
    order = [z, z - sign, z - 2 * sign, z - 3 * sign, z + sign, z + 2 * sign, z + 3 * sign, z + 4]
    cots = jnp.concatenate(
        [lax.dynamic_index_in_dim(all_cots, (place + 8) % 8, 0, False) for place in order], axis=0
    )

    own_router = lax.dynamic_index_in_dim(router.T, expert, 0, True)
    r_high, r_mid, r_low = split_three(own_router)
    logit = jnp.sum(
        contract_cols(inputs, jnp.concatenate((r_high, r_mid, r_low), 0)), axis=1, keepdims=True
    )
    gate = jax.nn.sigmoid(logit)
    pre_gate = jnp.dot(inputs, w_gate[0], preferred_element_type=F32)
    pre_up = jnp.dot(inputs, w_up[0], preferred_element_type=F32)
    sig = jax.nn.sigmoid(pre_gate)
    activated = (pre_gate * sig * pre_up).astype(BF)
    out_part = jnp.dot(activated, w_down[0], preferred_element_type=F32).astype(BF)
    out_cot = (gate * cots.astype(F32)).astype(BF)
    act_cot = contract_cols(out_cot, w_down[0])
    d_gate = (act_cot * pre_up * sig * (1.0 + pre_gate * (1.0 - sig))).astype(BF)
    d_up = (act_cot * pre_gate * sig).astype(BF)
    gate_term = (1.0 - gate) * jnp.sum(activated.astype(F32) * act_cot, axis=1, keepdims=True)
    in_part = (
        contract_cols(d_gate, w_gate[0]) + contract_cols(d_up, w_up[0]) + gate_term * own_router
    ).astype(BF)
    grad_down = contract_rows(activated, out_cot).astype(BF)[None]

    def collect(part):
        parts = part.reshape(8, cap, width)
        far_sent = lax.dynamic_slice_in_dim(parts[7], (1 - core) * half_width, half_width, 1)
        far_kept = lax.dynamic_slice_in_dim(parts[7], core * half_width, half_width, 1)
        total = (far_kept.astype(F32) + swap_core(far_sent).astype(F32)).astype(BF)
        total = hop(total, 8, True).astype(F32)
        nothing = jnp.zeros_like(total)
        total = join_halves(core, total, nothing)
        for place in (3, 2, 1):
            total = total + parts[place].astype(F32) + swap_core(parts[place + 3]).astype(F32)
            total = hop(total.astype(BF), 8, True).astype(F32)
        total = (total + parts[0].astype(F32)).astype(BF)
        return total.astype(F32) + swap_core(total).astype(F32)

    half_out = collect(out_part)
    half_in = collect(in_part)

    own_gate = gate[:cap]
    mean_part = jnp.sum(half_in * own_rows.astype(F32), axis=1)
    mean_high = lax.reduce_precision(mean_part, 8, 7)
    mean_low = mean_part - mean_high
    scaled = (own_gate * half_out).astype(BF)
    both = jnp.concatenate((scaled, half_in.astype(BF)), axis=0)
    both = lax.dynamic_slice_in_dim(both, core * half_width, half_width, 1)
    both = jnp.transpose(both.reshape(2 * cap, 16, block), (1, 0, 2))
    means = jnp.concatenate((mean_high, mean_low, jnp.zeros((block - 2 * cap,), F32))).astype(BF)
    message = jnp.concatenate(
        (both, jnp.broadcast_to(means[None, None], (16, 16, block))), axis=1
    )
    got = exchange(message)
    places = jnp.arange(experts * cap, dtype=jnp.int32)
    spread = (
        (target[:, :1] == places[None, :]) | (target[:, 1:] == places[None, :])
    ).reshape(rows, experts, 1, cap)
    spread = jnp.broadcast_to(spread, (rows, experts, 2, cap)).reshape(rows, 16 * cap)
    mixture = jnp.dot(
        spread.astype(BF), got[:, :cap].reshape(16 * cap, block), preferred_element_type=F32
    )
    normed_cot = jnp.dot(
        spread.astype(BF),
        got[:, cap : 2 * cap].reshape(16 * cap, block),
        preferred_element_type=F32,
    )
    means = got[:, 2 * cap, :cap].astype(F32) + got[:, 2 * cap, cap : 2 * cap].astype(F32)
    inner = jnp.sum(spread.astype(F32) * means.reshape(1, 16 * cap), axis=1, keepdims=True)
    gain_here = lax.dynamic_slice_in_dim(norm_gain, first, block, 0)
    cot_here = lax.dynamic_slice_in_dim(cotangent, first, block, 1).astype(F32)
    layer_here = (hidden + mixture).astype(BF)
    cot_out = (
        cot_here
        + inv_rms * (normed_cot * gain_here)
        - inv_rms * inv_rms * hidden * (inner / width)
    ).astype(BF)
    joined = jnp.concatenate((layer_here, cot_out), axis=0)
    got = exchange(jnp.broadcast_to(joined[None], (16, 2 * rows, block)))
    layer_out, grad_mixer = finish(core, got, swap_core(got), out_proj)
    return (layer_out, grad_mixer, grad_down)


def solution(mesh):
    fine = Mesh(mesh.devices.reshape(8, 4, 2, 2, 2), ("dp", "y", "xh", "half", "group"))
    tensor = ("y", "xh", "half")
    plane = tensor + ("group",)
    slices = ("dp", "group")
    placed = (
        P("dp", None),
        P("dp", plane),
        P(plane, None),
        P(),
        P(),
        P("dp", None),
        P(tensor, None, slices),
        P(tensor, None, slices),
        P(tensor, slices, None),
        P("dp", None),
    )
    return jax.shard_map(
        on_device,
        mesh=fine,
        in_specs=placed,
        out_specs=(P("dp", None), P("dp", plane), P(tensor, slices, None)),
        check_vma=False,
    )
```

```python
import jax
import jax.numpy as jnp
from jax import lax
from jax.experimental import pallas as pl
from jax.experimental.pallas import tpu as pltpu
from jax.sharding import Mesh, PartitionSpec as P

BF = jnp.bfloat16
F32 = jnp.float32
CHIPS = ("y", "xh", "half")


def contract_rows(left, right):
    return lax.dot_general(left, right, (((0,), (0,)), ((), ())), preferred_element_type=F32)


def contract_cols(left, right):
    return lax.dot_general(left, right, (((1,), (1,)), ((), ())), preferred_element_type=F32)


def split_three(values):
    high = lax.reduce_precision(values, 8, 7)
    rest = values - high
    mid = lax.reduce_precision(rest, 8, 7)
    low = rest - mid
    return high.astype(BF), mid.astype(BF), low.astype(BF)


def swap_core(value):
    return lax.ppermute(value, "group", [(0, 1), (1, 0)])


def hop(value, size, back):
    pairs = []
    for z in range(size):
        up, down = (z + 1) % size, (z - 1) % size
        if back:
            up, down = down, up
        pairs += [(2 * z, 2 * up), (2 * z + 1, 2 * down + 1)]
    return lax.ppermute(value, ("dp", "group"), pairs)


def exchange(blocks):
    return lax.all_to_all(blocks, CHIPS, 0, 0)


def join_halves(core, mine, other):
    return jnp.where(
        core == 0, jnp.concatenate((mine, other), 1), jnp.concatenate((other, mine), 1)
    )


def gather_features(core, block):
    rows, width = block.shape
    got = exchange(jnp.broadcast_to(block[None], (16, rows, width)))
    other = swap_core(got)
    mine = jnp.transpose(got, (1, 0, 2)).reshape(rows, 16 * width)
    other = jnp.transpose(other, (1, 0, 2)).reshape(rows, 16 * width)
    return join_halves(core, mine, other)


def finish_kernel(core_ref, mine_ref, other_ref, proj_ref, layer_ref, grad_ref, cot_ref, total_ref):
    rows, width = layer_ref.shape
    block = mine_ref.shape[2]
    core = core_ref[0]
    half = width // 2

    def place(chip, carry):
        for ref, number in ((mine_ref, core), (other_ref, 1 - core)):
            start = pl.multiple_of(number * half + chip * block, block)
            layer_ref[:, pl.ds(start, block)] = ref[chip, :rows]
            cot_ref[:, pl.ds(start, block)] = ref[chip, rows:]
        return carry

    lax.fori_loop(0, 16, place, 0)
    total_ref[...] = jnp.zeros_like(total_ref)

    def multiply(part, carry):
        columns = pl.ds(pl.multiple_of(part * 1024, 1024), 1024)
        total_ref[...] += contract_cols(cot_ref[:, columns], proj_ref[:, columns])
        return carry

    lax.fori_loop(0, width // 1024, multiply, 0)
    grad_ref[...] = total_ref[...].astype(BF)


def finish(core, mine, other, out_proj):
    rows = mine.shape[1] // 2
    channels, width = out_proj.shape
    vmem = pl.BlockSpec(memory_space=pltpu.VMEM)
    return pl.pallas_call(
        finish_kernel,
        out_shape=(
            jax.ShapeDtypeStruct((rows, width), BF),
            jax.ShapeDtypeStruct((rows, channels), BF),
        ),
        in_specs=[pl.BlockSpec(memory_space=pltpu.SMEM), vmem, vmem, vmem],
        out_specs=(vmem, vmem),
        scratch_shapes=[pltpu.VMEM((rows, width), BF), pltpu.VMEM((rows, channels), F32)],
        compiler_params=pltpu.CompilerParams(vmem_limit_bytes=32 * 1024 * 1024),
    )(core.reshape(1), mine, other, out_proj)


def on_device(
    resid, mixer_out, out_proj, norm_gain, router, routes, w_gate, w_up, w_down, cotangent
):
    rows, width = resid.shape
    experts = router.shape[1]
    units = w_gate.shape[2]
    cap = min(rows, 3 * rows // experts)
    half_width = width // 2
    block = half_width // 16
    z = lax.axis_index("dp")
    core = lax.axis_index("group")
    chip = (lax.axis_index("y") * 2 + lax.axis_index("xh")) * 2 + lax.axis_index("half")
    expert = lax.axis_index("y") * 2 + lax.axis_index("xh")
    first = core * half_width + chip * block

    pair_expert = routes.reshape(-1)
    onehot = (pair_expert[:, None] == jnp.arange(experts, dtype=jnp.int32)[None, :])
    before = jnp.dot(
        (jnp.arange(2 * rows)[:, None] > jnp.arange(2 * rows)[None, :]).astype(BF),
        onehot.astype(BF),
        preferred_element_type=F32,
    )
    slot = jnp.sum(before * onehot.astype(F32), axis=1).astype(jnp.int32)
    target = (pair_expert * cap + slot).reshape(rows, 2)
    own_slots = expert * cap + jnp.arange(cap, dtype=jnp.int32)
    select = (
        (target[None, :, 0] == own_slots[:, None]) | (target[None, :, 1] == own_slots[:, None])
    ).astype(BF)

    cot_half = lax.dynamic_slice_in_dim(cotangent, core * half_width, half_width, 1)
    own_cots = jnp.dot(select, cot_half, preferred_element_type=F32).astype(BF)
    mixer_out, own_cots = lax.optimization_barrier((mixer_out, own_cots))
    all_cots = lax.all_gather(own_cots, ("dp", "group"), axis=0).reshape(8, 2, cap, half_width)
    term = jnp.dot(mixer_out, out_proj, preferred_element_type=F32).astype(BF)
    sent = lax.dynamic_slice_in_dim(term, (1 - core) * half_width, half_width, 1)
    kept = lax.dynamic_slice_in_dim(term, core * half_width, half_width, 1)
    chip_term = (kept.astype(F32) + swap_core(sent).astype(F32)).astype(BF)
    blocks = exchange(jnp.transpose(chip_term.reshape(rows, 16, block), (1, 0, 2)))
    hidden = lax.dynamic_slice_in_dim(resid, first, block, 1).astype(F32) + jnp.sum(
        blocks.astype(F32), axis=0
    )
    whole = gather_features(core, hidden.astype(BF)).astype(F32)
    inv_rms = lax.rsqrt(jnp.mean(whole * whole, axis=1, keepdims=True) + 1e-05)
    normed = (whole * inv_rms * norm_gain).astype(BF)
    own_rows = jnp.dot(select, normed, preferred_element_type=F32).astype(BF)

    own_rows, all_cots = lax.optimization_barrier((own_rows, all_cots))
    near = [own_rows]
    for _ in range(3):
        near.append(hop(near[-1], 8, False))
    far = hop(
        lax.dynamic_slice_in_dim(near[3], core * half_width, half_width, 1), 8, False
    )
    others = [swap_core(value) for value in near[1:]]
    far = join_halves(core, far, swap_core(far))
    inputs = jnp.concatenate(near + others + [far], axis=0)
    sign = 1 - 2 * core
    order = [z, z - sign, z - 2 * sign, z - 3 * sign, z + sign, z + 2 * sign, z + 3 * sign, z + 4]
    cots = [lax.dynamic_index_in_dim(all_cots, (place + 8) % 8, 0, False) for place in order]
    cots = jnp.concatenate(
        [jnp.concatenate((value[0], value[1]), axis=1) for value in cots], axis=0
    )

    own_router = lax.dynamic_index_in_dim(router.T, expert, 0, True)
    r_high, r_mid, r_low = split_three(own_router)
    logit = jnp.sum(
        contract_cols(inputs, jnp.concatenate((r_high, r_mid, r_low), 0)), axis=1, keepdims=True
    )
    gate = jax.nn.sigmoid(logit)
    pre_gate = jnp.dot(inputs, w_gate[0], preferred_element_type=F32)
    pre_up = jnp.dot(inputs, w_up[0], preferred_element_type=F32)
    sig = jax.nn.sigmoid(pre_gate)
    activated = (pre_gate * sig * pre_up).astype(BF)
    out_part = jnp.dot(activated, w_down[0], preferred_element_type=F32).astype(BF)
    out_cot = (gate * cots.astype(F32)).astype(BF)
    act_cot = contract_cols(out_cot, w_down[0])
    d_gate = (act_cot * pre_up * sig * (1.0 + pre_gate * (1.0 - sig))).astype(BF)
    d_up = (act_cot * pre_gate * sig).astype(BF)
    gate_term = (1.0 - gate) * jnp.sum(activated.astype(F32) * act_cot, axis=1, keepdims=True)
    in_part = (
        contract_cols(d_gate, w_gate[0]) + contract_cols(d_up, w_up[0]) + gate_term * own_router
    ).astype(BF)
    grad_down = contract_rows(activated, out_cot).astype(BF)[None]

    def collect(part):
        parts = part.reshape(8, cap, width)
        far_sent = lax.dynamic_slice_in_dim(parts[7], (1 - core) * half_width, half_width, 1)
        far_kept = lax.dynamic_slice_in_dim(parts[7], core * half_width, half_width, 1)
        total = (far_kept.astype(F32) + swap_core(far_sent).astype(F32)).astype(BF)
        total = hop(total, 8, True).astype(F32)
        nothing = jnp.zeros_like(total)
        total = join_halves(core, total, nothing)
        for place in (3, 2, 1):
            total = total + parts[place].astype(F32) + swap_core(parts[place + 3]).astype(F32)
            total = hop(total.astype(BF), 8, True).astype(F32)
        total = (total + parts[0].astype(F32)).astype(BF)
        return total.astype(F32) + swap_core(total).astype(F32)

    half_out = collect(out_part)
    half_in = collect(in_part)

    own_gate = gate[:cap]
    mean_part = jnp.sum(half_in * own_rows.astype(F32), axis=1)
    mean_high = lax.reduce_precision(mean_part, 8, 7)
    mean_low = mean_part - mean_high
    scaled = (own_gate * half_out).astype(BF)
    both = jnp.concatenate((scaled, half_in.astype(BF)), axis=0)
    both = lax.dynamic_slice_in_dim(both, core * half_width, half_width, 1)
    both = jnp.transpose(both.reshape(2 * cap, 16, block), (1, 0, 2))
    means = jnp.concatenate((mean_high, mean_low, jnp.zeros((block - 2 * cap,), F32))).astype(BF)
    message = jnp.concatenate(
        (both, jnp.broadcast_to(means[None, None], (16, 16, block))), axis=1
    )
    got = exchange(message)
    places = jnp.arange(experts * cap, dtype=jnp.int32)
    spread = (
        (target[:, :1] == places[None, :]) | (target[:, 1:] == places[None, :])
    ).reshape(rows, experts, 1, cap)
    spread = jnp.broadcast_to(spread, (rows, experts, 2, cap)).reshape(rows, 16 * cap)
    mixture = jnp.dot(
        spread.astype(BF), got[:, :cap].reshape(16 * cap, block), preferred_element_type=F32
    )
    normed_cot = jnp.dot(
        spread.astype(BF),
        got[:, cap : 2 * cap].reshape(16 * cap, block),
        preferred_element_type=F32,
    )
    means = got[:, 2 * cap, :cap].astype(F32) + got[:, 2 * cap, cap : 2 * cap].astype(F32)
    inner = jnp.sum(spread.astype(F32) * means.reshape(1, 16 * cap), axis=1, keepdims=True)
    gain_here = lax.dynamic_slice_in_dim(norm_gain, first, block, 0)
    cot_here = lax.dynamic_slice_in_dim(cotangent, first, block, 1).astype(F32)
    layer_here = (hidden + mixture).astype(BF)
    cot_out = (
        cot_here
        + inv_rms * (normed_cot * gain_here)
        - inv_rms * inv_rms * hidden * (inner / width)
    ).astype(BF)
    joined = jnp.concatenate((layer_here, cot_out), axis=0)
    got = exchange(jnp.broadcast_to(joined[None], (16, 2 * rows, block)))
    layer_out, grad_mixer = finish(core, got, swap_core(got), out_proj)
    return (layer_out, grad_mixer, grad_down)


def solution(mesh):
    fine = Mesh(mesh.devices.reshape(8, 4, 2, 2, 2), ("dp", "y", "xh", "half", "group"))
    tensor = ("y", "xh", "half")
    plane = tensor + ("group",)
    slices = ("dp", "group")
    placed = (
        P("dp", None),
        P("dp", plane),
        P(plane, None),
        P(),
        P(),
        P("dp", None),
        P(tensor, None, slices),
        P(tensor, None, slices),
        P(tensor, slices, None),
        P("dp", None),
    )
    return jax.shard_map(
        on_device,
        mesh=fine,
        in_specs=placed,
        out_specs=(P("dp", None), P("dp", plane), P(tensor, slices, None)),
        check_vma=False,
    )
```

```python
import jax
import jax.numpy as jnp
from jax import lax
from jax.experimental import pallas as pl
from jax.experimental.pallas import tpu as pltpu
from jax.sharding import Mesh, PartitionSpec as P

BF = jnp.bfloat16
F32 = jnp.float32
CHIPS = ("y", "xh", "half")


def contract_rows(left, right):
    return lax.dot_general(left, right, (((0,), (0,)), ((), ())), preferred_element_type=F32)


def contract_cols(left, right):
    return lax.dot_general(left, right, (((1,), (1,)), ((), ())), preferred_element_type=F32)


def split_three(values):
    high = lax.reduce_precision(values, 8, 7)
    rest = values - high
    mid = lax.reduce_precision(rest, 8, 7)
    low = rest - mid
    return high.astype(BF), mid.astype(BF), low.astype(BF)


def swap_core(value):
    return lax.ppermute(value, "group", [(0, 1), (1, 0)])


def hop(value, size, back):
    pairs = []
    for z in range(size):
        up, down = (z + 1) % size, (z - 1) % size
        if back:
            up, down = down, up
        pairs += [(2 * z, 2 * up), (2 * z + 1, 2 * down + 1)]
    return lax.ppermute(value, ("dp", "group"), pairs)


def exchange(blocks):
    return lax.all_to_all(blocks, CHIPS, 0, 0)


def join_halves(core, mine, other):
    return jnp.where(
        core == 0, jnp.concatenate((mine, other), 1), jnp.concatenate((other, mine), 1)
    )


def gather_features(core, block):
    rows, width = block.shape
    got = exchange(jnp.broadcast_to(block[None], (16, rows, width)))
    other = swap_core(got)
    mine = jnp.transpose(got, (1, 0, 2)).reshape(rows, 16 * width)
    other = jnp.transpose(other, (1, 0, 2)).reshape(rows, 16 * width)
    return join_halves(core, mine, other)


def finish_kernel(core_ref, mine_ref, other_ref, proj_ref, layer_ref, grad_ref, cot_ref, total_ref):
    rows, width = layer_ref.shape
    block = mine_ref.shape[2]
    core = core_ref[0]
    half = width // 2

    def place(chip, carry):
        for ref, number in ((mine_ref, core), (other_ref, 1 - core)):
            start = pl.multiple_of(number * half + chip * block, block)
            layer_ref[:, pl.ds(start, block)] = ref[chip, :rows]
            cot_ref[:, pl.ds(start, block)] = ref[chip, rows:]
        return carry

    lax.fori_loop(0, 16, place, 0)
    total_ref[...] = jnp.zeros_like(total_ref)

    def multiply(part, carry):
        columns = pl.ds(pl.multiple_of(part * 1024, 1024), 1024)
        total_ref[...] += contract_cols(cot_ref[:, columns], proj_ref[:, columns])
        return carry

    lax.fori_loop(0, width // 1024, multiply, 0)
    grad_ref[...] = total_ref[...].astype(BF)


def finish(core, mine, other, out_proj):
    rows = mine.shape[1] // 2
    channels, width = out_proj.shape
    vmem = pl.BlockSpec(memory_space=pltpu.VMEM)
    return pl.pallas_call(
        finish_kernel,
        out_shape=(
            jax.ShapeDtypeStruct((rows, width), BF),
            jax.ShapeDtypeStruct((rows, channels), BF),
        ),
        in_specs=[pl.BlockSpec(memory_space=pltpu.SMEM), vmem, vmem, vmem],
        out_specs=(vmem, vmem),
        scratch_shapes=[pltpu.VMEM((rows, width), BF), pltpu.VMEM((rows, channels), F32)],
        compiler_params=pltpu.CompilerParams(vmem_limit_bytes=32 * 1024 * 1024),
    )(core.reshape(1), mine, other, out_proj)


def on_device(
    resid, mixer_out, out_proj, norm_gain, router, routes, w_gate, w_up, w_down, cotangent
):
    rows, width = resid.shape
    experts = router.shape[1]
    units = w_gate.shape[2]
    cap = min(rows, 3 * rows // experts)
    half_width = width // 2
    block = half_width // 16
    z = lax.axis_index("dp")
    core = lax.axis_index("group")
    chip = (lax.axis_index("y") * 2 + lax.axis_index("xh")) * 2 + lax.axis_index("half")
    expert = lax.axis_index("y") * 2 + lax.axis_index("xh")
    first = core * half_width + chip * block

    pair_expert = routes.reshape(-1)
    onehot = (pair_expert[:, None] == jnp.arange(experts, dtype=jnp.int32)[None, :])
    before = jnp.dot(
        (jnp.arange(2 * rows)[:, None] > jnp.arange(2 * rows)[None, :]).astype(BF),
        onehot.astype(BF),
        preferred_element_type=F32,
    )
    slot = jnp.sum(before * onehot.astype(F32), axis=1).astype(jnp.int32)
    target = (pair_expert * cap + slot).reshape(rows, 2)
    own_slots = expert * cap + jnp.arange(cap, dtype=jnp.int32)
    select = (
        (target[None, :, 0] == own_slots[:, None]) | (target[None, :, 1] == own_slots[:, None])
    ).astype(BF)

    cot_half = lax.dynamic_slice_in_dim(cotangent, core * half_width, half_width, 1)
    own_cots = jnp.dot(select, cot_half, preferred_element_type=F32).astype(BF)
    mixer_out, own_cots = lax.optimization_barrier((mixer_out, own_cots))
    all_cots = lax.all_gather(own_cots, ("dp", "group"), axis=0).reshape(8, 2, cap, half_width)
    term = jnp.dot(mixer_out, out_proj, preferred_element_type=F32).astype(BF)
    sent = lax.dynamic_slice_in_dim(term, (1 - core) * half_width, half_width, 1)
    kept = lax.dynamic_slice_in_dim(term, core * half_width, half_width, 1)
    chip_term = (kept.astype(F32) + swap_core(sent).astype(F32)).astype(BF)
    blocks = exchange(jnp.transpose(chip_term.reshape(rows, 16, block), (1, 0, 2)))
    hidden = lax.dynamic_slice_in_dim(resid, first, block, 1).astype(F32) + jnp.sum(
        blocks.astype(F32), axis=0
    )
    whole = gather_features(core, hidden.astype(BF)).astype(F32)
    inv_rms = lax.rsqrt(jnp.mean(whole * whole, axis=1, keepdims=True) + 1e-05)
    normed = (whole * inv_rms * norm_gain).astype(BF)
    own_rows = jnp.dot(select, normed, preferred_element_type=F32).astype(BF)

    own_rows, all_cots = lax.optimization_barrier((own_rows, all_cots))
    near = [own_rows]
    for _ in range(3):
        near.append(hop(near[-1], 8, False))
    far = hop(
        lax.dynamic_slice_in_dim(near[3], core * half_width, half_width, 1), 8, False
    )
    others = [swap_core(value) for value in near[1:]]
    far = join_halves(core, far, swap_core(far))
    inputs = jnp.concatenate(near + others + [far], axis=0)
    sign = 1 - 2 * core
    order = [z, z - sign, z - 2 * sign, z - 3 * sign, z + sign, z + 2 * sign, z + 3 * sign, z + 4]
    cots = [lax.dynamic_index_in_dim(all_cots, (place + 8) % 8, 0, False) for place in order]
    cots = jnp.concatenate(
        [jnp.concatenate((value[0], value[1]), axis=1) for value in cots], axis=0
    )

    own_router = lax.dynamic_index_in_dim(router.T, expert, 0, True)
    r_high, r_mid, r_low = split_three(own_router)
    logit = jnp.sum(
        contract_cols(inputs, jnp.concatenate((r_high, r_mid, r_low), 0)), axis=1, keepdims=True
    )
    gate = jax.nn.sigmoid(logit)
    pre_gate = jnp.dot(inputs, w_gate[0], preferred_element_type=F32)
    pre_up = jnp.dot(inputs, w_up[0], preferred_element_type=F32)
    sig = jax.nn.sigmoid(pre_gate)
    activated = (pre_gate * sig * pre_up).astype(BF)
    out_part = jnp.dot(activated, w_down[0], preferred_element_type=F32).astype(BF)
    out_cot = (gate * cots.astype(F32)).astype(BF)
    act_cot = contract_cols(out_cot, w_down[0])
    d_gate = (act_cot * pre_up * sig * (1.0 + pre_gate * (1.0 - sig))).astype(BF)
    d_up = (act_cot * pre_gate * sig).astype(BF)
    gate_term = (1.0 - gate) * jnp.sum(activated.astype(F32) * act_cot, axis=1, keepdims=True)
    in_part = (
        contract_cols(d_gate, w_gate[0]) + contract_cols(d_up, w_up[0]) + gate_term * own_router
    ).astype(BF)
    grad_down = contract_rows(activated, out_cot).astype(BF)[None]

    def collect(part):
        parts = part.reshape(8, cap, width)
        far_sent = lax.dynamic_slice_in_dim(parts[7], (1 - core) * half_width, half_width, 1)
        far_kept = lax.dynamic_slice_in_dim(parts[7], core * half_width, half_width, 1)
        total = (far_kept.astype(F32) + swap_core(far_sent).astype(F32)).astype(BF)
        total = hop(total, 8, True).astype(F32)
        nothing = jnp.zeros_like(total)
        total = join_halves(core, total, nothing)
        for place in (3, 2, 1):
            total = total + parts[place].astype(F32) + swap_core(parts[place + 3]).astype(F32)
            total = hop(total.astype(BF), 8, True).astype(F32)
        total = (total + parts[0].astype(F32)).astype(BF)
        return total.astype(F32) + swap_core(total).astype(F32)

    half_out = collect(out_part)
    half_in = collect(in_part)
    half_in, grad_down = lax.optimization_barrier((half_in, grad_down))

    own_gate = gate[:cap]
    mean_part = jnp.sum(half_in * own_rows.astype(F32), axis=1)
    mean_high = lax.reduce_precision(mean_part, 8, 7)
    mean_low = mean_part - mean_high
    scaled = (own_gate * half_out).astype(BF)
    both = jnp.concatenate((scaled, half_in.astype(BF)), axis=0)
    both = lax.dynamic_slice_in_dim(both, core * half_width, half_width, 1)
    both = jnp.transpose(both.reshape(2 * cap, 16, block), (1, 0, 2))
    means = jnp.concatenate((mean_high, mean_low, jnp.zeros((block - 2 * cap,), F32))).astype(BF)
    message = jnp.concatenate(
        (both, jnp.broadcast_to(means[None, None], (16, 16, block))), axis=1
    )
    got = exchange(message)
    places = jnp.arange(experts * cap, dtype=jnp.int32)
    spread = (
        (target[:, :1] == places[None, :]) | (target[:, 1:] == places[None, :])
    ).reshape(rows, experts, 1, cap)
    spread = jnp.broadcast_to(spread, (rows, experts, 2, cap)).reshape(rows, 16 * cap)
    mixture = jnp.dot(
        spread.astype(BF), got[:, :cap].reshape(16 * cap, block), preferred_element_type=F32
    )
    normed_cot = jnp.dot(
        spread.astype(BF),
        got[:, cap : 2 * cap].reshape(16 * cap, block),
        preferred_element_type=F32,
    )
    means = got[:, 2 * cap, :cap].astype(F32) + got[:, 2 * cap, cap : 2 * cap].astype(F32)
    inner = jnp.sum(spread.astype(F32) * means.reshape(1, 16 * cap), axis=1, keepdims=True)
    gain_here = lax.dynamic_slice_in_dim(norm_gain, first, block, 0)
    cot_here = lax.dynamic_slice_in_dim(cotangent, first, block, 1).astype(F32)
    layer_here = (hidden + mixture).astype(BF)
    cot_out = (
        cot_here
        + inv_rms * (normed_cot * gain_here)
        - inv_rms * inv_rms * hidden * (inner / width)
    ).astype(BF)
    joined = jnp.concatenate((layer_here, cot_out), axis=0)
    got = exchange(jnp.broadcast_to(joined[None], (16, 2 * rows, block)))
    layer_out, grad_mixer = finish(core, got, swap_core(got), out_proj)
    return (layer_out, grad_mixer, grad_down)


def solution(mesh):
    fine = Mesh(mesh.devices.reshape(8, 4, 2, 2, 2), ("dp", "y", "xh", "half", "group"))
    tensor = ("y", "xh", "half")
    plane = tensor + ("group",)
    slices = ("dp", "group")
    placed = (
        P("dp", None),
        P("dp", plane),
        P(plane, None),
        P(),
        P(),
        P("dp", None),
        P(tensor, None, slices),
        P(tensor, None, slices),
        P(tensor, slices, None),
        P("dp", None),
    )
    return jax.shard_map(
        on_device,
        mesh=fine,
        in_specs=placed,
        out_specs=(P("dp", None), P("dp", plane), P(tensor, slices, None)),
        check_vma=False,
    )
```
